32 devices in a mesh: hst: 8 (over z, x), local: 4 (over y, core).
Axes of the slice: x: 2, y: 2, z: 4, core: 2. Of those that a mesh axis runs over, the one named last changes fastest.
Arguments:
- patches: bfloat16 [32768, 768], P(('hst', 'local')), may hold values from -6 to 6
- w_in: bfloat16 [768, 3072], replicated, may hold values from -0.21875 to 0.21875
- b_in: float32 [3072], replicated, may hold values from -3 to 3
- w_out: bfloat16 [3072, 512], replicated, may hold values from -0.15625 to 0.15625
- b_out: float32 [512], replicated, may hold values from -3 to 3
- ema_sums: float32 [32768, 512], P(('hst', 'local')), may hold values from -12 to 12
- ema_counts: float32 [32768], P(('hst', 'local')), may hold values from 0.5 to 4
- code_ids: int32 [32768], P(('hst', 'local')), may hold values from 0 to 32767, as said below
Outputs:
- codebook: float32 [32768, 512], P(('hst', 'local'))
- new_counts: float32 [32768], P(('hst', 'local'))
- quantized: bfloat16 [32768, 512], P(('hst', 'local'))
The draws below stay inside these ranges and needn't reach their ends.
Inputs may be any that keep to these rules, and one draw needn't show every extreme that they name: `code_ids`: in each aligned block of 1024 patches (the patches of one device), at most 64 ids lie in any one range [k * 1024, (k + 1) * 1024); one such range gets exactly 64 from every block.
All inputs are finite; a program needn't handle non-finite values.
Results may differ from the reference program's by a relative error of at most 0.002.
Values may be sent and summed in bfloat16 or wider, within the bound.
A program may use at most 64 MiB of HBM per device.

```python
import math
import jax
import jax.numpy as jnp
from jax import lax

D_IN = 768
HIDDEN_SIZE = 3072
D_LAT = 512
CODES_DEV = 1024
P_DEV = 1024
OWNERS = 32
CAP = 64
PATCHES = 32768
CODES = 32768


def draw_code_ids(key, part):
    slot_total = OWNERS * CAP
    hot_owner = jax.random.randint(jax.random.fold_in(key, 1), (), 0, OWNERS)
    owner_weight = jax.random.randint(jax.random.fold_in(key, 2), (OWNERS,), 0, 1024)
    slot_owner = jnp.arange(slot_total) // CAP
    slot_number = jnp.arange(slot_total)

    def one_source(src_key):
        base_score = jax.random.randint(jax.random.fold_in(src_key, 3), (slot_total,), 0, 1024)
        score = (base_score + owner_weight[slot_owner]) * slot_total + slot_number
        score = jnp.where(slot_owner == hot_owner, -1 - slot_number, score)
        unused, picked = lax.top_k(score, P_DEV - CAP)
        row_owner = jnp.concatenate([jnp.full((CAP,), hot_owner, jnp.int32), slot_owner[picked].astype(jnp.int32)])
        row_owner = jax.random.permutation(jax.random.fold_in(src_key, 4), row_owner)
        exponent = jax.random.randint(jax.random.fold_in(src_key, 5), (P_DEV,), 0, 11)
        limit = jnp.minimum(jnp.power(2, exponent), CODES_DEV)
        offsets = jax.random.randint(jax.random.fold_in(src_key, 6), (P_DEV,), 0, limit)
        return row_owner * CODES_DEV + offsets
    source_keys = jax.random.split(jax.random.fold_in(key, 9), OWNERS)
    return jax.vmap(one_source)(source_keys).reshape(-1).astype(jnp.int32)


def steps_of(stream_key, extent, cuts, least, top_value):
    level, own = 1.0, jax.random.fold_in(stream_key, 6)
    for axis_at, blocks in cuts:
        draws = jnp.exp(jax.random.uniform(jax.random.fold_in(own, axis_at), (blocks,), jnp.float32, least / len(cuts), top_value / len(cuts)))
        level = level * jnp.repeat(draws, extent[axis_at] // blocks).reshape([-1 if axis == axis_at else 1 for axis in range(len(extent))])
    return level


def gaussian(key, dims, deviation, most, cuts=(), held_as=jnp.bfloat16):
    entries = deviation * jax.random.normal(key, dims, jnp.float32)
    if cuts:
        entries = entries * steps_of(key, dims, cuts, -0.22, 0.18)
    return jnp.clip(entries, -most, most).astype(held_as)


def setup_inputs(seed: int = 0) -> dict:
    arg_keys = jax.random.split(jax.random.key(seed), 9)
    patches = gaussian(arg_keys[0], (PATCHES, D_IN), 1.0, 6.0, ((0, 32),))
    w_in = gaussian(arg_keys[1], (D_IN, HIDDEN_SIZE), D_IN ** -0.5, 0.21875)
    b_in = gaussian(arg_keys[2], (HIDDEN_SIZE,), 0.5, 3.0, (), jnp.float32)
    w_out = gaussian(arg_keys[3], (HIDDEN_SIZE, D_LAT), (HIDDEN_SIZE // 2) ** -0.5, 0.15625)
    b_out = gaussian(arg_keys[4], (D_LAT,), 0.5, 3.0, (), jnp.float32)
    ema_sums = gaussian(arg_keys[5], (CODES, D_LAT), 2.0, 12.0, ((0, 32),), jnp.float32)
    ema_counts = jnp.clip(jnp.exp(math.log(4.0) - 2.0794415 * jax.random.uniform(arg_keys[6], (CODES,), jnp.float32) ** steps_of(arg_keys[6], (CODES,), ((0, 32),), -0.2, 0.2)), 0.5, 4.0)
    code_ids = draw_code_ids(jax.random.fold_in(arg_keys[8], 71), 0)
    return dict(patches=patches, w_in=w_in, b_in=b_in, w_out=w_out, b_out=b_out, ema_sums=ema_sums, ema_counts=ema_counts, code_ids=code_ids)


DECAY = 0.9


def reference(patches, w_in, b_in, w_out, b_out, ema_sums, ema_counts, code_ids):
    grouped = patches.reshape(OWNERS, P_DEV, D_IN)

    def encode(row_block):
        pre_act = jnp.dot(row_block, w_in, preferred_element_type=jnp.float32) + b_in
        hidden = jnp.tanh(pre_act).astype(jnp.bfloat16)
        latent = jnp.dot(hidden, w_out, preferred_element_type=jnp.float32) + b_out
        return latent.astype(jnp.bfloat16)

    latents = lax.map(encode, grouped).reshape(PATCHES, D_LAT)
    code_sums = jax.ops.segment_sum(latents.astype(jnp.float32), code_ids, num_segments=CODES)
    code_counts = jax.ops.segment_sum(jnp.ones((PATCHES,), jnp.float32), code_ids, num_segments=CODES)
    new_counts = DECAY * ema_counts + (1.0 - DECAY) * code_counts
    codebook = (DECAY * ema_sums + (1.0 - DECAY) * code_sums) / new_counts[:, None]
    quantized = codebook.astype(jnp.bfloat16)[code_ids]
    return codebook, new_counts, quantized
```

```python
import functools

import jax
import jax.numpy as jnp
from jax import lax
from jax.experimental import pallas as pl
from jax.experimental.pallas import tpu as pltpu
from jax.sharding import PartitionSpec as P

DECAY = 0.9
CHUNKS = 2
MESH = pl.DeviceIdType.MESH
F32 = jnp.float32
BF16 = jnp.bfloat16


def iota(shape, dim):
    return lax.broadcasted_iota(jnp.int32, shape, dim)


def to_column(row):
    eye = iota((128, 128), 0) == iota((128, 128), 1)
    return jnp.sum(jnp.where(eye, jnp.broadcast_to(row, (128, 128)), 0.0), axis=1, keepdims=True)


def one_hot(mask):
    return jnp.where(mask, 1.0, 0.0).astype(BF16)


def dot_nt(a, b):
    return lax.dot_general(a, b, (((1,), (1,)), ((), ())), preferred_element_type=F32)


def kernel(
    hosts, locals_, capacity,
    patches_hbm, w_in_hbm, b_in, w_out_hbm, b_out, ema_hbm, counts_row, ids_row,
    codebook, new_counts_row, quantized,
    patches, w_in, w_out, ema, hidden, latents, placing, unplacing, chosen, chosen_t, scale,
    ids_out, ids_in, out, arrived, replies, back,
    load_sem, ids_send, ids_recv, send_a, recv_a, send_b, recv_b,
):
    owners = hosts * locals_
    rows = patches.shape[0]
    span, width = ema.shape
    chunk = width // CHUNKS
    slots = owners * capacity
    group = 128 // capacity
    my_host, my_local = lax.axis_index("hst"), lax.axis_index("local")
    me = my_host * locals_ + my_local
    stride = max(1, hosts // 2 - 1)

    def peer(step):
        host = lax.rem(my_host + stride * (lax.rem(step, hosts) + 1), hosts)
        local = lax.rem(my_local + step // hosts + 1, locals_)
        return host, local

    def each_peer(body):
        def run(step, carry):
            host, local = peer(step)
            body(host, local, host * locals_ + local)
            return carry
        lax.fori_loop(0, owners - 1, run, 0)

    loads = [
        pltpu.make_async_copy(src, dst, load_sem.at[at])
        for at, (src, dst) in enumerate(
            ((patches_hbm, patches), (w_in_hbm, w_in), (w_out_hbm, w_out), (ema_hbm, ema))
        )
    ]
    for load in loads:
        load.start()
    barrier = pltpu.get_barrier_semaphore()
    each_peer(
        lambda host, local, rank: pl.semaphore_signal(
            barrier, inc=1, device_id=(host, local), device_id_type=MESH
        )
    )

    ids = ids_row[...]
    owner = ids // span
    members = iota((owners, rows), 0) == owner
    before = one_hot(iota((rows, rows), 0) <= iota((rows, rows), 1))
    running = jnp.dot(one_hot(members), before, preferred_element_type=F32)
    position = jnp.sum(jnp.where(members, running, 0.0), axis=0, keepdims=True) - 1.0
    position = position.astype(jnp.int32)
    slot = owner * capacity + position
    block = min(slots, 256)

    def fill_placing(at, carry):
        start = pl.multiple_of(at * block, block)
        placing[pl.ds(start, block), :] = one_hot(iota((block, rows), 0) + start == slot)
        return carry
    lax.fori_loop(0, slots // block, fill_placing, 0)

    code = ids - owner * span + 1
    high, low = (code // 128).astype(F32), lax.rem(code, 128).astype(F32)
    part = lax.rem(iota((owners * 8, rows), 0), 8)
    value = jnp.where(part == 0, high, jnp.where(part == 1, low, 0.0))
    sending = jnp.where(iota((owners * 8, rows), 0) // 8 == owner, value, 0.0).astype(BF16)
    lane = position + capacity * lax.rem(me, group)
    lanes = one_hot(iota((128, rows), 0) == lane)
    ids_out[...] = dot_nt(sending, lanes).reshape(owners, 8, 128)
    ids_in[pl.ds(me, 1)] = ids_out[pl.ds(me, 1)]

    loads[0].wait()
    loads[1].wait()
    tile = 512

    def first_layer(at, carry):
        columns = pl.ds(pl.multiple_of(at * tile, tile), tile)
        pre_act = jnp.dot(patches[...], w_in[:, columns], preferred_element_type=F32)
        hidden[:, columns] = jnp.tanh(pre_act + b_in[:, columns]).astype(BF16)
        return carry
    lax.fori_loop(0, hidden.shape[1] // tile, first_layer, 0)
    loads[2].wait()

    def ids_copy(host, local, rank, slot_at):
        return pltpu.make_async_remote_copy(
            src_ref=ids_out.at[rank], dst_ref=ids_in.at[slot_at], send_sem=ids_send.at[rank],
            recv_sem=ids_recv.at[slot_at], device_id=(host, local), device_id_type=MESH,
        )

    def rows_copy(at, source, target, send, recv, host, local, rank, slot_at):
        return pltpu.make_async_remote_copy(
            src_ref=source.at[at, rank], dst_ref=target.at[at, slot_at], send_sem=send.at[at, rank],
            recv_sem=recv.at[at, slot_at], device_id=(host, local), device_id_type=MESH,
        )

    def send_latents(at):
        columns = slice(at * chunk, (at + 1) * chunk)
        latent = jnp.dot(hidden[...], w_out[:, columns], preferred_element_type=F32)
        latents[...] = (latent + b_out[:, columns]).astype(BF16)

        def pack(piece, carry):
            some = pl.ds(pl.multiple_of(piece * block, block), block)
            packed = jnp.dot(placing[some, :], latents[...], preferred_element_type=F32)
            count = block // capacity
            out[at, pl.ds(piece * count, count)] = packed.astype(BF16).reshape(
                count, capacity, chunk
            )
            return carry
        lax.fori_loop(0, slots // block, pack, 0)
        if at == 0:
            pl.semaphore_wait(barrier, owners - 1)
            each_peer(lambda host, local, rank: ids_copy(host, local, rank, me).start())
        each_peer(
            lambda host, local, rank: rows_copy(
                at, out, arrived, send_a, recv_a, host, local, rank, me
            ).start()
        )
        arrived[at, pl.ds(me, 1)] = out[at, pl.ds(me, 1)]

    for at in range(CHUNKS):
        send_latents(at)

    for at in range(rows // 128):
        column = to_column(slot[:, at * 128:(at + 1) * 128].astype(F32)).astype(jnp.int32)
        unplacing[at * 128:(at + 1) * 128, :] = one_hot(iota((128, slots), 1) == column)

    each_peer(lambda host, local, rank: ids_copy(host, local, rank, rank).wait_recv())
    for at in range(slots // 128):
        codes = jnp.zeros((1, 128), F32)
        for source in range(at * group, (at + 1) * group):
            codes = codes + ids_in[source, 0:1, :] * 128.0 + ids_in[source, 1:2, :]
        column = to_column(codes).astype(jnp.int32)
        chosen[at * 128:(at + 1) * 128, :] = one_hot(iota((128, span), 1) + 1 == column)
        chosen_t[:, at * 128:(at + 1) * 128] = one_hot(
            iota((span, 128), 0) + 1 == codes.astype(jnp.int32)
        )
    counts = jnp.dot(jnp.ones((8, slots), BF16), chosen[...], preferred_element_type=F32)[0:1]
    new_counts = DECAY * counts_row[...] + (1.0 - DECAY) * counts
    new_counts_row[...] = new_counts
    for at in range(span // 128):
        scale[at * 128:(at + 1) * 128, :] = jnp.broadcast_to(
            to_column(new_counts[:, at * 128:(at + 1) * 128]), (128, 128)
        )
    loads[3].wait()

    for at in range(CHUNKS):
        columns = slice(at * chunk, (at + 1) * chunk)
        each_peer(
            lambda host, local, rank: rows_copy(
                at, out, arrived, send_a, recv_a, host, local, rank, rank
            ).wait_recv()
        )
        sums = jnp.dot(
            chosen_t[...], arrived[at].reshape(slots, chunk), preferred_element_type=F32
        )
        book = (DECAY * ema[:, columns] + (1.0 - DECAY) * sums) / scale[:, 0:1]
        codebook[:, columns] = book
        latents[...] = book.astype(BF16)

        def reply(piece, carry):
            some = pl.ds(pl.multiple_of(piece * block, block), block)
            found = jnp.dot(chosen[some, :], latents[...], preferred_element_type=F32)
            count = block // capacity
            replies[at, pl.ds(piece * count, count)] = found.astype(BF16).reshape(
                count, capacity, chunk
            )
            return carry
        lax.fori_loop(0, slots // block, reply, 0)
        each_peer(
            lambda host, local, rank: rows_copy(
                at, replies, back, send_b, recv_b, host, local, rank, me
            ).start()
        )
        back[at, pl.ds(me, 1)] = replies[at, pl.ds(me, 1)]

    for at in range(CHUNKS):
        columns = slice(at * chunk, (at + 1) * chunk)
        each_peer(
            lambda host, local, rank: rows_copy(
                at, replies, back, send_b, recv_b, host, local, rank, rank
            ).wait_recv()
        )
        quantized[:, columns] = jnp.dot(
            unplacing[...], back[at].reshape(slots, chunk), preferred_element_type=F32
        ).astype(BF16)

    each_peer(lambda host, local, rank: ids_copy(host, local, rank, rank).wait_send())
    for at in range(CHUNKS):
        each_peer(
            lambda host, local, rank: rows_copy(
                at, out, arrived, send_a, recv_a, host, local, rank, rank
            ).wait_send()
        )
        each_peer(
            lambda host, local, rank: rows_copy(
                at, replies, back, send_b, recv_b, host, local, rank, rank
            ).wait_send()
        )


def fused(hosts, locals_, capacity, patches, w_in, b_in, w_out, b_out, ema_sums, ema_counts, code_ids):
    owners = hosts * locals_
    rows, depth = patches.shape
    span, width = ema_sums.shape
    hidden = w_in.shape[1]
    chunk = width // CHUNKS
    slots = owners * capacity
    vmem = pl.BlockSpec(memory_space=pltpu.VMEM)
    hbm = pl.BlockSpec(memory_space=pl.ANY)
    traded = pltpu.VMEM((CHUNKS, owners, capacity, chunk), BF16)
    dma = pltpu.SemaphoreType.DMA
    flops = 2 * rows * hidden * (depth + width) + 8 * slots * rows * width
    codebook, new_counts, quantized = pl.pallas_call(
        functools.partial(kernel, hosts, locals_, capacity),
        out_shape=(
            jax.ShapeDtypeStruct((span, width), F32),
            jax.ShapeDtypeStruct((1, span), F32),
            jax.ShapeDtypeStruct((rows, width), BF16),
        ),
        in_specs=[hbm, hbm, vmem, hbm, vmem, hbm, vmem, vmem],
        out_specs=(vmem, vmem, vmem),
        scratch_shapes=[
            pltpu.VMEM((rows, depth), BF16),
            pltpu.VMEM((depth, hidden), BF16),
            pltpu.VMEM((hidden, width), BF16),
            pltpu.VMEM((span, width), F32),
            pltpu.VMEM((rows, hidden), BF16),
            pltpu.VMEM((max(rows, span), chunk), BF16),
            pltpu.VMEM((slots, rows), BF16),
            pltpu.VMEM((rows, slots), BF16),
            pltpu.VMEM((slots, span), BF16),
            pltpu.VMEM((span, slots), BF16),
            pltpu.VMEM((span, 128), F32),
            pltpu.VMEM((owners, 8, 128), F32),
            pltpu.VMEM((owners, 8, 128), F32),
            traded, traded, traded, traded,
            dma((4,)), dma((owners,)), dma((owners,)),
            dma((CHUNKS, owners)), dma((CHUNKS, owners)),
            dma((CHUNKS, owners)), dma((CHUNKS, owners)),
        ],
        compiler_params=pltpu.CompilerParams(
            collective_id=0, has_side_effects=True, vmem_limit_bytes=60 * 2**20
        ),
        cost_estimate=pl.CostEstimate(
            flops=flops, bytes_accessed=14 * 2**20, transcendentals=rows * hidden
        ),
    )(
        patches, w_in, b_in.reshape(1, -1), w_out, b_out.reshape(1, -1), ema_sums,
        ema_counts.reshape(1, -1), code_ids.reshape(1, -1),
    )
    return codebook, new_counts.reshape(span), quantized


def staged(patches, w_in, b_in, w_out, b_out, ema_sums, ema_counts, code_ids):
    host_count = lax.axis_size("hst")
    local_count = lax.axis_size("local")
    owner_count = host_count * local_count
    code_span = ema_sums.shape[0]
    latent_width = ema_sums.shape[1]
    row_count = patches.shape[0]
    capacity = max(2, 2 * row_count // owner_count)
    pre_act = jnp.dot(patches, w_in, preferred_element_type=jnp.float32) + b_in
    hidden = jnp.tanh(pre_act).astype(jnp.bfloat16)
    latents = (jnp.dot(hidden, w_out, preferred_element_type=jnp.float32) + b_out).astype(
        jnp.bfloat16
    )
    owner_of = code_ids // code_span
    members = (owner_of[:, None] == jnp.arange(owner_count)[None, :]).astype(jnp.int32)
    running = jnp.cumsum(members, axis=0)
    position = jnp.sum(running * members, axis=1) - 1
    slot_index = owner_of * capacity + position
    placing = jnp.arange(owner_count * capacity)[:, None] == slot_index[None, :]
    outgoing = jnp.dot(
        placing.astype(jnp.bfloat16), latents, preferred_element_type=jnp.float32
    ).astype(jnp.bfloat16)
    sent_ids = jnp.max(jnp.where(placing, code_ids[None, :], -1), axis=1)
    outgoing = outgoing.reshape(host_count, local_count, capacity, latent_width)
    sent_ids = sent_ids.reshape(host_count, local_count, capacity)
    halfway = (
        lax.all_to_all(outgoing, "hst", split_axis=0, concat_axis=0, tiled=True),
        lax.all_to_all(sent_ids, "hst", split_axis=0, concat_axis=0, tiled=True),
    )
    arrived, arrived_ids = (
        lax.all_to_all(halfway[0], "local", split_axis=1, concat_axis=1, tiled=True),
        lax.all_to_all(halfway[1], "local", split_axis=1, concat_axis=1, tiled=True),
    )
    arrived = arrived.reshape(owner_count * capacity, latent_width)
    arrived_ids = arrived_ids.reshape(owner_count * capacity)
    first_code = (lax.axis_index("hst") * local_count + lax.axis_index("local")) * code_span
    offset_code = arrived_ids - first_code
    chosen = (offset_code[:, None] == jnp.arange(code_span)[None, :]).astype(jnp.bfloat16)
    code_sums = lax.dot_general(
        chosen, arrived, (((0,), (0,)), ((), ())), preferred_element_type=jnp.float32
    )
    code_counts = jnp.sum(chosen, axis=0, dtype=jnp.float32)
    new_counts = DECAY * ema_counts + (1.0 - DECAY) * code_counts
    codebook = (DECAY * ema_sums + (1.0 - DECAY) * code_sums) / new_counts[:, None]
    replies = jnp.dot(
        chosen, codebook.astype(jnp.bfloat16), preferred_element_type=jnp.float32
    ).astype(jnp.bfloat16)
    replies = replies.reshape(host_count, local_count, capacity, latent_width)
    returned = lax.all_to_all(
        lax.all_to_all(replies, "hst", split_axis=0, concat_axis=0, tiled=True),
        "local",
        split_axis=1,
        concat_axis=1,
        tiled=True,
    )
    back_rows = returned.reshape(owner_count * capacity, latent_width)
    quantized = jnp.take(back_rows, slot_index, axis=0)
    return (codebook, new_counts, quantized)


def per_device(patches, w_in, b_in, w_out, b_out, ema_sums, ema_counts, code_ids):
    hosts, locals_ = lax.axis_size("hst"), lax.axis_size("local")
    rows, span = patches.shape[0], ema_sums.shape[0]
    capacity = max(2, 2 * rows // (hosts * locals_))
    if capacity % 16 or 128 % capacity or rows != span:
        return staged(patches, w_in, b_in, w_out, b_out, ema_sums, ema_counts, code_ids)
    return fused(
        hosts, locals_, capacity,
        patches, w_in, b_in, w_out, b_out, ema_sums, ema_counts, code_ids,
    )


def solution(mesh):
    in_specs = (
        P(("hst", "local"), None),
        P(),
        P(),
        P(),
        P(),
        P(("hst", "local"), None),
        P(("hst", "local")),
        P(("hst", "local")),
    )
    out_specs = (P(("hst", "local"), None), P(("hst", "local")), P(("hst", "local"), None))
    return jax.shard_map(
        per_device, mesh=mesh, in_specs=in_specs, out_specs=out_specs, check_vma=False
    )
```

```python
import functools
import math

import jax
import jax.numpy as jnp
from jax import lax
from jax.experimental import pallas as pl
from jax.experimental.pallas import tpu as pltpu
from jax.sharding import PartitionSpec as P

DECAY = 0.9
CHUNKS = 2
MESH = pl.DeviceIdType.MESH
F32 = jnp.float32
BF16 = jnp.bfloat16


def iota(shape, dim):
    return lax.broadcasted_iota(jnp.int32, shape, dim)


def to_column(row):
    eye = iota((128, 128), 0) == iota((128, 128), 1)
    return jnp.sum(jnp.where(eye, jnp.broadcast_to(row, (128, 128)), 0.0), axis=1, keepdims=True)


def one_hot(mask):
    return jnp.where(mask, 1.0, 0.0).astype(BF16)


def dot_nt(a, b):
    return lax.dot_general(a, b, (((1,), (1,)), ((), ())), preferred_element_type=F32)


def kernel(
    hosts, locals_, capacity,
    patches_hbm, w_in_hbm, b_in, w_out_hbm, b_out, ema_hbm, counts_row, ids_row,
    codebook_hbm, new_counts_row, quantized,
    codebook, patches, w_in, w_out, ema, hidden, latents, placing, unplacing, chosen, chosen_t, scale,
    ids_out, ids_in, out, arrived, replies, back,
    load_sem, store_sem, ids_send, ids_recv, send_a, recv_a, send_b, recv_b,
):
    owners = hosts * locals_
    rows = patches.shape[0]
    span, width = ema.shape
    chunk = width // CHUNKS
    slots = owners * capacity
    group = 128 // capacity
    my_host, my_local = lax.axis_index("hst"), lax.axis_index("local")
    me = my_host * locals_ + my_local
    stride = next(k for k in range(max(1, hosts // 2 - 1), hosts + 1) if math.gcd(k, hosts) == 1)

    def each_peer(body):
        for ahead in range(1, locals_ + 1):
            local = my_local + ahead
            local = jnp.where(local >= locals_, local - locals_, local)

            def run(step, host):
                host = host + stride
                host = jnp.where(host >= hosts, host - hosts, host)
                body(host, local, host * locals_ + local)
                return host
            lax.fori_loop(0, hosts - (ahead == locals_), run, my_host)

    loads = [
        pltpu.make_async_copy(src, dst, load_sem.at[at])
        for at, (src, dst) in enumerate(
            ((patches_hbm, patches), (w_in_hbm, w_in), (w_out_hbm, w_out), (ema_hbm, ema))
        )
    ]
    for load in loads:
        load.start()
    barrier = pltpu.get_barrier_semaphore()
    each_peer(
        lambda host, local, rank: pl.semaphore_signal(
            barrier, inc=1, device_id=(host, local), device_id_type=MESH
        )
    )

    ids = ids_row[...]
    owner = ids // span
    members = iota((owners, rows), 0) == owner
    before = one_hot(iota((rows, rows), 0) <= iota((rows, rows), 1))
    running = jnp.dot(one_hot(members), before, preferred_element_type=F32)
    position = jnp.sum(jnp.where(members, running, 0.0), axis=0, keepdims=True) - 1.0
    position = position.astype(jnp.int32)
    slot = owner * capacity + position
    block = min(slots, 256)

    def fill_placing(at, carry):
        start = pl.multiple_of(at * block, block)
        placing[pl.ds(start, block), :] = one_hot(iota((block, rows), 0) + start == slot)
        return carry
    lax.fori_loop(0, slots // block, fill_placing, 0)

    code = ids - owner * span + 1
    high, low = (code // 128).astype(F32), lax.rem(code, 128).astype(F32)
    line = iota((owners * 8, rows), 0) - owner * 8
    sending = jnp.where(line == 0, high, jnp.where(line == 1, low, 0.0)).astype(BF16)
    lane = position + capacity * lax.rem(me, group)
    lanes = one_hot(iota((128, rows), 0) == lane)
    ids_out[...] = dot_nt(sending, lanes).reshape(owners, 8, 128)
    ids_in[pl.ds(me, 1)] = ids_out[pl.ds(me, 1)]

    loads[0].wait()
    loads[1].wait()
    tile = 512

    def first_layer(at, carry):
        columns = pl.ds(pl.multiple_of(at * tile, tile), tile)
        pre_act = jnp.dot(patches[...], w_in[:, columns], preferred_element_type=F32)
        hidden[:, columns] = jnp.tanh((pre_act + b_in[:, columns]).astype(BF16))
        return carry
    lax.fori_loop(0, hidden.shape[1] // tile, first_layer, 0)
    loads[2].wait()

    def ids_copy(host, local, rank, slot_at):
        return pltpu.make_async_remote_copy(
            src_ref=ids_out.at[rank], dst_ref=ids_in.at[slot_at], send_sem=ids_send.at[rank],
            recv_sem=ids_recv.at[slot_at], device_id=(host, local), device_id_type=MESH,
        )

    def rows_copy(at, source, target, send, recv, host, local, rank, slot_at):
        return pltpu.make_async_remote_copy(
            src_ref=source.at[at, rank], dst_ref=target.at[at, slot_at], send_sem=send.at[at, rank],
            recv_sem=recv.at[at, slot_at], device_id=(host, local), device_id_type=MESH,
        )

    def send_latents(at):
        columns = slice(at * chunk, (at + 1) * chunk)
        latent = jnp.dot(hidden[...], w_out[:, columns], preferred_element_type=F32)
        latents[...] = (latent + b_out[:, columns]).astype(BF16)

        def pack(piece, carry):
            some = pl.ds(pl.multiple_of(piece * block, block), block)
            packed = jnp.dot(placing[some, :], latents[...], preferred_element_type=F32)
            count = block // capacity
            out[at, pl.ds(piece * count, count)] = packed.astype(BF16).reshape(
                count, capacity, chunk
            )
            return carry
        lax.fori_loop(0, slots // block, pack, 0)
        if at == 0:
            pl.semaphore_wait(barrier, owners - 1)
            each_peer(lambda host, local, rank: ids_copy(host, local, rank, me).start())
        each_peer(
            lambda host, local, rank: rows_copy(
                at, out, arrived, send_a, recv_a, host, local, rank, me
            ).start()
        )
        arrived[at, pl.ds(me, 1)] = out[at, pl.ds(me, 1)]

    for at in range(CHUNKS):
        send_latents(at)

    for at in range(rows // 128):
        column = to_column(slot[:, at * 128:(at + 1) * 128].astype(F32)).astype(jnp.int32)
        unplacing[at * 128:(at + 1) * 128, :] = one_hot(iota((128, slots), 1) == column)

    each_peer(lambda host, local, rank: ids_copy(host, local, rank, rank).wait_recv())
    for at in range(slots // 128):
        codes = jnp.zeros((1, 128), F32)
        for source in range(at * group, (at + 1) * group):
            codes = codes + ids_in[source, 0:1, :] * 128.0 + ids_in[source, 1:2, :]
        column = to_column(codes).astype(jnp.int32)
        chosen[at * 128:(at + 1) * 128, :] = one_hot(iota((128, span), 1) + 1 == column)
        chosen_t[:, at * 128:(at + 1) * 128] = one_hot(
            iota((span, 128), 0) + 1 == codes.astype(jnp.int32)
        )
    counts = jnp.dot(jnp.ones((8, slots), BF16), chosen[...], preferred_element_type=F32)[0:1]
    new_counts = DECAY * counts_row[...] + (1.0 - DECAY) * counts
    new_counts_row[...] = new_counts
    for at in range(span // 128):
        scale[at * 128:(at + 1) * 128, :] = jnp.broadcast_to(
            to_column(new_counts[:, at * 128:(at + 1) * 128]), (128, 128)
        )
    loads[3].wait()

    for at in range(CHUNKS):
        columns = slice(at * chunk, (at + 1) * chunk)
        each_peer(
            lambda host, local, rank: rows_copy(
                at, out, arrived, send_a, recv_a, host, local, rank, rank
            ).wait_recv()
        )
        sums = jnp.dot(
            chosen_t[...], arrived[at].reshape(slots, chunk), preferred_element_type=F32
        )
        book = (DECAY * ema[:, columns] + (1.0 - DECAY) * sums) / scale[:, 0:1]
        codebook[at] = book
        pltpu.make_async_copy(
            codebook.at[at], codebook_hbm.at[:, columns], store_sem.at[at]
        ).start()
        latents[...] = book.astype(BF16)

        def reply(piece, carry):
            some = pl.ds(pl.multiple_of(piece * block, block), block)
            found = jnp.dot(chosen[some, :], latents[...], preferred_element_type=F32)
            count = block // capacity
            replies[at, pl.ds(piece * count, count)] = found.astype(BF16).reshape(
                count, capacity, chunk
            )
            return carry
        lax.fori_loop(0, slots // block, reply, 0)
        each_peer(
            lambda host, local, rank: rows_copy(
                at, replies, back, send_b, recv_b, host, local, rank, me
            ).start()
        )
        back[at, pl.ds(me, 1)] = replies[at, pl.ds(me, 1)]

    for at in range(CHUNKS):
        columns = slice(at * chunk, (at + 1) * chunk)
        each_peer(
            lambda host, local, rank: rows_copy(
                at, replies, back, send_b, recv_b, host, local, rank, rank
            ).wait_recv()
        )
        quantized[:, columns] = jnp.dot(
            unplacing[...], back[at].reshape(slots, chunk), preferred_element_type=F32
        ).astype(BF16)

    each_peer(lambda host, local, rank: ids_copy(host, local, rank, rank).wait_send())
    for at in range(CHUNKS):
        columns = slice(at * chunk, (at + 1) * chunk)
        pltpu.make_async_copy(
            codebook.at[at], codebook_hbm.at[:, columns], store_sem.at[at]
        ).wait()
    for at in range(CHUNKS):
        each_peer(
            lambda host, local, rank: rows_copy(
                at, out, arrived, send_a, recv_a, host, local, rank, rank
            ).wait_send()
        )
        each_peer(
            lambda host, local, rank: rows_copy(
                at, replies, back, send_b, recv_b, host, local, rank, rank
            ).wait_send()
        )


def fused(hosts, locals_, capacity, patches, w_in, b_in, w_out, b_out, ema_sums, ema_counts, code_ids):
    owners = hosts * locals_
    rows, depth = patches.shape
    span, width = ema_sums.shape
    hidden = w_in.shape[1]
    chunk = width // CHUNKS
    slots = owners * capacity
    vmem = pl.BlockSpec(memory_space=pltpu.VMEM)
    hbm = pl.BlockSpec(memory_space=pl.ANY)
    traded = pltpu.VMEM((CHUNKS, owners, capacity, chunk), BF16)
    dma = pltpu.SemaphoreType.DMA
    flops = 2 * rows * hidden * (depth + width) + 8 * slots * rows * width
    codebook, new_counts, quantized = pl.pallas_call(
        functools.partial(kernel, hosts, locals_, capacity),
        out_shape=(
            jax.ShapeDtypeStruct((span, width), F32),
            jax.ShapeDtypeStruct((1, span), F32),
            jax.ShapeDtypeStruct((rows, width), BF16),
        ),
        in_specs=[hbm, hbm, vmem, hbm, vmem, hbm, vmem, vmem],
        out_specs=(hbm, vmem, vmem),
        scratch_shapes=[
            pltpu.VMEM((CHUNKS, span, chunk), F32),
            pltpu.VMEM((rows, depth), BF16),
            pltpu.VMEM((depth, hidden), BF16),
            pltpu.VMEM((hidden, width), BF16),
            pltpu.VMEM((span, width), F32),
            pltpu.VMEM((rows, hidden), BF16),
            pltpu.VMEM((max(rows, span), chunk), BF16),
            pltpu.VMEM((slots, rows), BF16),
            pltpu.VMEM((rows, slots), BF16),
            pltpu.VMEM((slots, span), BF16),
            pltpu.VMEM((span, slots), BF16),
            pltpu.VMEM((span, 128), F32),
            pltpu.VMEM((owners, 8, 128), F32),
            pltpu.VMEM((owners, 8, 128), F32),
            traded, traded, traded, traded,
            dma((4,)), dma((CHUNKS,)), dma((owners,)), dma((owners,)),
            dma((CHUNKS, owners)), dma((CHUNKS, owners)),
            dma((CHUNKS, owners)), dma((CHUNKS, owners)),
        ],
        compiler_params=pltpu.CompilerParams(
            collective_id=0, has_side_effects=True, vmem_limit_bytes=60 * 2**20
        ),
        cost_estimate=pl.CostEstimate(
            flops=flops, bytes_accessed=14 * 2**20, transcendentals=rows * hidden
        ),
    )(
        patches, w_in, b_in.reshape(1, -1), w_out, b_out.reshape(1, -1), ema_sums,
        ema_counts.reshape(1, -1), code_ids.reshape(1, -1),
    )
    return codebook, new_counts.reshape(span), quantized


def staged(patches, w_in, b_in, w_out, b_out, ema_sums, ema_counts, code_ids):
    host_count = lax.axis_size("hst")
    local_count = lax.axis_size("local")
    owner_count = host_count * local_count
    code_span = ema_sums.shape[0]
    latent_width = ema_sums.shape[1]
    row_count = patches.shape[0]
    capacity = max(2, 2 * row_count // owner_count)
    pre_act = jnp.dot(patches, w_in, preferred_element_type=jnp.float32) + b_in
    hidden = jnp.tanh(pre_act).astype(jnp.bfloat16)
    latents = (jnp.dot(hidden, w_out, preferred_element_type=jnp.float32) + b_out).astype(
        jnp.bfloat16
    )
    owner_of = code_ids // code_span
    members = (owner_of[:, None] == jnp.arange(owner_count)[None, :]).astype(jnp.int32)
    running = jnp.cumsum(members, axis=0)
    position = jnp.sum(running * members, axis=1) - 1
    slot_index = owner_of * capacity + position
    placing = jnp.arange(owner_count * capacity)[:, None] == slot_index[None, :]
    outgoing = jnp.dot(
        placing.astype(jnp.bfloat16), latents, preferred_element_type=jnp.float32
    ).astype(jnp.bfloat16)
    sent_ids = jnp.max(jnp.where(placing, code_ids[None, :], -1), axis=1)
    outgoing = outgoing.reshape(host_count, local_count, capacity, latent_width)
    sent_ids = sent_ids.reshape(host_count, local_count, capacity)
    halfway = (
        lax.all_to_all(outgoing, "hst", split_axis=0, concat_axis=0, tiled=True),
        lax.all_to_all(sent_ids, "hst", split_axis=0, concat_axis=0, tiled=True),
    )
    arrived, arrived_ids = (
        lax.all_to_all(halfway[0], "local", split_axis=1, concat_axis=1, tiled=True),
        lax.all_to_all(halfway[1], "local", split_axis=1, concat_axis=1, tiled=True),
    )
    arrived = arrived.reshape(owner_count * capacity, latent_width)
    arrived_ids = arrived_ids.reshape(owner_count * capacity)
    first_code = (lax.axis_index("hst") * local_count + lax.axis_index("local")) * code_span
    offset_code = arrived_ids - first_code
    chosen = (offset_code[:, None] == jnp.arange(code_span)[None, :]).astype(jnp.bfloat16)
    code_sums = lax.dot_general(
        chosen, arrived, (((0,), (0,)), ((), ())), preferred_element_type=jnp.float32
    )
    code_counts = jnp.sum(chosen, axis=0, dtype=jnp.float32)
    new_counts = DECAY * ema_counts + (1.0 - DECAY) * code_counts
    codebook = (DECAY * ema_sums + (1.0 - DECAY) * code_sums) / new_counts[:, None]
    replies = jnp.dot(
        chosen, codebook.astype(jnp.bfloat16), preferred_element_type=jnp.float32
    ).astype(jnp.bfloat16)
    replies = replies.reshape(host_count, local_count, capacity, latent_width)
    returned = lax.all_to_all(
        lax.all_to_all(replies, "hst", split_axis=0, concat_axis=0, tiled=True),
        "local",
        split_axis=1,
        concat_axis=1,
        tiled=True,
    )
    back_rows = returned.reshape(owner_count * capacity, latent_width)
    quantized = jnp.take(back_rows, slot_index, axis=0)
    return (codebook, new_counts, quantized)


def per_device(patches, w_in, b_in, w_out, b_out, ema_sums, ema_counts, code_ids):
    hosts, locals_ = lax.axis_size("hst"), lax.axis_size("local")
    rows, span = patches.shape[0], ema_sums.shape[0]
    capacity = max(2, 2 * rows // (hosts * locals_))
    if capacity % 16 or 128 % capacity or rows != span:
        return staged(patches, w_in, b_in, w_out, b_out, ema_sums, ema_counts, code_ids)
    return fused(
        hosts, locals_, capacity,
        patches, w_in, b_in, w_out, b_out, ema_sums, ema_counts, code_ids,
    )


def solution(mesh):
    in_specs = (
        P(("hst", "local"), None),
        P(),
        P(),
        P(),
        P(),
        P(("hst", "local"), None),
        P(("hst", "local")),
        P(("hst", "local")),
    )
    out_specs = (P(("hst", "local"), None), P(("hst", "local")), P(("hst", "local"), None))
    return jax.shard_map(
        per_device, mesh=mesh, in_specs=in_specs, out_specs=out_specs, check_vma=False
    )
```

```python
import functools
import math

import jax
import jax.numpy as jnp
from jax import lax
from jax.experimental import pallas as pl
from jax.experimental.pallas import tpu as pltpu
from jax.sharding import PartitionSpec as P

DECAY = 0.9
CHUNKS = 4
DEPTH = 2
MESH = pl.DeviceIdType.MESH
F32 = jnp.float32
BF16 = jnp.bfloat16


def iota(shape, dim):
    return lax.broadcasted_iota(jnp.int32, shape, dim)


def to_column(row):
    eye = iota((128, 128), 0) == iota((128, 128), 1)
    return jnp.sum(jnp.where(eye, jnp.broadcast_to(row, (128, 128)), 0.0), axis=1, keepdims=True)


def one_hot(mask):
    return jnp.where(mask, 1.0, 0.0).astype(BF16)


def dot_nt(a, b):
    return lax.dot_general(a, b, (((1,), (1,)), ((), ())), preferred_element_type=F32)


def kernel(
    hosts, locals_, capacity,
    patches_hbm, w_in_hbm, b_in, w_out_hbm, b_out, ema_hbm, counts_row, ids_row,
    codebook, new_counts_row, quantized,
    patches, w_in, w_out, ema, hidden, latents, placing, unplacing, chosen, chosen_t, scale,
    ids_out, ids_in, out, arrived, replies, back,
    load_sem, ids_send, ids_recv, send_a, recv_a, send_b, recv_b,
):
    owners = hosts * locals_
    rows = patches.shape[0]
    span, width = ema.shape
    chunk = width // CHUNKS
    slots = owners * capacity
    group = 128 // capacity
    my_host, my_local = lax.axis_index("hst"), lax.axis_index("local")
    me = my_host * locals_ + my_local
    stride = next(k for k in range(max(1, hosts // 2 - 1), hosts + 1) if math.gcd(k, hosts) == 1)

    def each_peer(body):
        for ahead in range(1, locals_ + 1):
            local = my_local + ahead
            local = jnp.where(local >= locals_, local - locals_, local)

            def run(step, host):
                host = host + stride
                host = jnp.where(host >= hosts, host - hosts, host)
                body(host, local, host * locals_ + local)
                return host
            lax.fori_loop(0, hosts - (ahead == locals_), run, my_host)

    loads = [
        pltpu.make_async_copy(src, dst, load_sem.at[at])
        for at, (src, dst) in enumerate(
            ((patches_hbm, patches), (w_in_hbm, w_in), (w_out_hbm, w_out), (ema_hbm, ema))
        )
    ]
    for load in loads:
        load.start()
    barrier = pltpu.get_barrier_semaphore()
    each_peer(
        lambda host, local, rank: pl.semaphore_signal(
            barrier, inc=1, device_id=(host, local), device_id_type=MESH
        )
    )

    ids = ids_row[...]
    owner = ids // span
    members = iota((owners, rows), 0) == owner
    before = one_hot(iota((rows, rows), 0) <= iota((rows, rows), 1))
    running = jnp.dot(one_hot(members), before, preferred_element_type=F32)
    position = jnp.sum(jnp.where(members, running, 0.0), axis=0, keepdims=True) - 1.0
    position = position.astype(jnp.int32)
    slot = owner * capacity + position
    block = min(slots, 256)

    def fill_placing(at, carry):
        start = pl.multiple_of(at * block, block)
        placing[pl.ds(start, block), :] = one_hot(iota((block, rows), 0) + start == slot)
        return carry
    lax.fori_loop(0, slots // block, fill_placing, 0)

    code = ids - owner * span + 1
    high, low = (code // 128).astype(F32), lax.rem(code, 128).astype(F32)
    line = iota((owners * 8, rows), 0) - owner * 8
    sending = jnp.where(line == 0, high, jnp.where(line == 1, low, 0.0)).astype(BF16)
    lane = position + capacity * lax.rem(me, group)
    lanes = one_hot(iota((128, rows), 0) == lane)
    ids_out[...] = dot_nt(sending, lanes).reshape(owners, 8, 128)
    ids_in[pl.ds(me, 1)] = ids_out[pl.ds(me, 1)]

    loads[0].wait()
    loads[1].wait()
    tile = 512

    def first_layer(at, carry):
        columns = pl.ds(pl.multiple_of(at * tile, tile), tile)
        pre_act = jnp.dot(patches[...], w_in[:, columns], preferred_element_type=F32)
        hidden[:, columns] = jnp.tanh((pre_act + b_in[:, columns]).astype(BF16))
        return carry
    lax.fori_loop(0, hidden.shape[1] // tile, first_layer, 0)
    loads[2].wait()

    def ids_copy(host, local, rank, slot_at):
        return pltpu.make_async_remote_copy(
            src_ref=ids_out.at[rank], dst_ref=ids_in.at[slot_at], send_sem=ids_send.at[rank],
            recv_sem=ids_recv.at[slot_at], device_id=(host, local), device_id_type=MESH,
        )

    def rows_copy(turn, host, local, rank, slot_at):
        at = turn % CHUNKS
        source, target, send, recv = (
            (out, arrived, send_a, recv_a) if turn < CHUNKS else (replies, back, send_b, recv_b)
        )
        return pltpu.make_async_remote_copy(
            src_ref=source.at[at, rank], dst_ref=target.at[at, slot_at], send_sem=send.at[at, rank],
            recv_sem=recv.at[at, slot_at], device_id=(host, local), device_id_type=MESH,
        )

    def start_turn(turn):
        def start(host, local, rank):
            if turn >= DEPTH:
                rows_copy(turn - DEPTH, host, local, rank, rank).wait_send()
            rows_copy(turn, host, local, rank, me).start()
        each_peer(start)

    def wait_turn(turn):
        each_peer(
            lambda host, local, rank: rows_copy(turn, host, local, rank, rank).wait_recv()
        )

    def send_latents(at):
        columns = slice(at * chunk, (at + 1) * chunk)
        latent = jnp.dot(hidden[...], w_out[:, columns], preferred_element_type=F32)
        latents[...] = (latent + b_out[:, columns]).astype(BF16)

        def pack(piece, carry):
            some = pl.ds(pl.multiple_of(piece * block, block), block)
            packed = jnp.dot(placing[some, :], latents[...], preferred_element_type=F32)
            count = block // capacity
            out[at, pl.ds(piece * count, count)] = packed.astype(BF16).reshape(
                count, capacity, chunk
            )
            return carry
        lax.fori_loop(0, slots // block, pack, 0)
        if at == 0:
            pl.semaphore_wait(barrier, owners - 1)
            each_peer(lambda host, local, rank: ids_copy(host, local, rank, me).start())
        start_turn(at)
        arrived[at, pl.ds(me, 1)] = out[at, pl.ds(me, 1)]

    for at in range(DEPTH):
        send_latents(at)

    for at in range(rows // 128):
        column = to_column(slot[:, at * 128:(at + 1) * 128].astype(F32)).astype(jnp.int32)
        unplacing[at * 128:(at + 1) * 128, :] = one_hot(iota((128, slots), 1) == column)

    each_peer(lambda host, local, rank: ids_copy(host, local, rank, rank).wait_recv())
    for at in range(slots // 128):
        codes = jnp.zeros((1, 128), F32)
        for source in range(at * group, (at + 1) * group):
            codes = codes + ids_in[source, 0:1, :] * 128.0 + ids_in[source, 1:2, :]
        column = to_column(codes).astype(jnp.int32)
        chosen[at * 128:(at + 1) * 128, :] = one_hot(iota((128, span), 1) + 1 == column)
        chosen_t[:, at * 128:(at + 1) * 128] = one_hot(
            iota((span, 128), 0) + 1 == codes.astype(jnp.int32)
        )
    counts = jnp.dot(jnp.ones((8, slots), BF16), chosen[...], preferred_element_type=F32)[0:1]
    new_counts = DECAY * counts_row[...] + (1.0 - DECAY) * counts
    new_counts_row[...] = new_counts
    for at in range(span // 128):
        scale[at * 128:(at + 1) * 128, :] = jnp.broadcast_to(
            to_column(new_counts[:, at * 128:(at + 1) * 128]), (128, 128)
        )
    loads[3].wait()

    for at in range(DEPTH, CHUNKS):
        send_latents(at)

    for at in range(CHUNKS):
        columns = slice(at * chunk, (at + 1) * chunk)
        wait_turn(at)
        sums = jnp.dot(
            chosen_t[...], arrived[at].reshape(slots, chunk), preferred_element_type=F32
        )
        book = (DECAY * ema[:, columns] + (1.0 - DECAY) * sums) / scale[:, 0:1]
        codebook[:, columns] = book
        latents[...] = book.astype(BF16)

        def reply(piece, carry):
            some = pl.ds(pl.multiple_of(piece * block, block), block)
            found = jnp.dot(chosen[some, :], latents[...], preferred_element_type=F32)
            count = block // capacity
            replies[at, pl.ds(piece * count, count)] = found.astype(BF16).reshape(
                count, capacity, chunk
            )
            return carry
        lax.fori_loop(0, slots // block, reply, 0)
        start_turn(CHUNKS + at)
        back[at, pl.ds(me, 1)] = replies[at, pl.ds(me, 1)]

    for at in range(CHUNKS):
        columns = slice(at * chunk, (at + 1) * chunk)
        wait_turn(CHUNKS + at)
        quantized[:, columns] = jnp.dot(
            unplacing[...], back[at].reshape(slots, chunk), preferred_element_type=F32
        ).astype(BF16)

    each_peer(lambda host, local, rank: ids_copy(host, local, rank, rank).wait_send())
    for turn in range(2 * CHUNKS - DEPTH, 2 * CHUNKS):
        each_peer(
            lambda host, local, rank: rows_copy(turn, host, local, rank, rank).wait_send()
        )


def fused(hosts, locals_, capacity, patches, w_in, b_in, w_out, b_out, ema_sums, ema_counts, code_ids):
    owners = hosts * locals_
    rows, depth = patches.shape
    span, width = ema_sums.shape
    hidden = w_in.shape[1]
    chunk = width // CHUNKS
    slots = owners * capacity
    vmem = pl.BlockSpec(memory_space=pltpu.VMEM)
    hbm = pl.BlockSpec(memory_space=pl.ANY)
    traded = pltpu.VMEM((CHUNKS, owners, capacity, chunk), BF16)
    dma = pltpu.SemaphoreType.DMA
    flops = 2 * rows * hidden * (depth + width) + 8 * slots * rows * width
    codebook, new_counts, quantized = pl.pallas_call(
        functools.partial(kernel, hosts, locals_, capacity),
        out_shape=(
            pltpu.VMEM((span, width), F32),
            jax.ShapeDtypeStruct((1, span), F32),
            pltpu.VMEM((rows, width), BF16),
        ),
        in_specs=[hbm, hbm, vmem, hbm, vmem, hbm, vmem, vmem],
        out_specs=(vmem, vmem, vmem),
        scratch_shapes=[
            pltpu.VMEM((rows, depth), BF16),
            pltpu.VMEM((depth, hidden), BF16),
            pltpu.VMEM((hidden, width), BF16),
            pltpu.VMEM((span, width), F32),
            pltpu.VMEM((rows, hidden), BF16),
            pltpu.VMEM((max(rows, span), chunk), BF16),
            pltpu.VMEM((slots, rows), BF16),
            pltpu.VMEM((rows, slots), BF16),
            pltpu.VMEM((slots, span), BF16),
            pltpu.VMEM((span, slots), BF16),
            pltpu.VMEM((span, 128), F32),
            pltpu.VMEM((owners, 8, 128), F32),
            pltpu.VMEM((owners, 8, 128), F32),
            traded, traded, traded, traded,
            dma((4,)), dma((owners,)), dma((owners,)),
            dma((CHUNKS, owners)), dma((CHUNKS, owners)),
            dma((CHUNKS, owners)), dma((CHUNKS, owners)),
        ],
        compiler_params=pltpu.CompilerParams(
            collective_id=0, has_side_effects=True, vmem_limit_bytes=56 * 2**20
        ),
        cost_estimate=pl.CostEstimate(
            flops=flops, bytes_accessed=14 * 2**20, transcendentals=rows * hidden
        ),
    )(
        patches, w_in, b_in.reshape(1, -1), w_out, b_out.reshape(1, -1), ema_sums,
        ema_counts.reshape(1, -1), code_ids.reshape(1, -1),
    )
    return codebook, new_counts.reshape(span), quantized


def staged(patches, w_in, b_in, w_out, b_out, ema_sums, ema_counts, code_ids):
    host_count = lax.axis_size("hst")
    local_count = lax.axis_size("local")
    owner_count = host_count * local_count
    code_span = ema_sums.shape[0]
    latent_width = ema_sums.shape[1]
    row_count = patches.shape[0]
    capacity = max(2, 2 * row_count // owner_count)
    pre_act = jnp.dot(patches, w_in, preferred_element_type=jnp.float32) + b_in
    hidden = jnp.tanh(pre_act).astype(jnp.bfloat16)
    latents = (jnp.dot(hidden, w_out, preferred_element_type=jnp.float32) + b_out).astype(
        jnp.bfloat16
    )
    owner_of = code_ids // code_span
    members = (owner_of[:, None] == jnp.arange(owner_count)[None, :]).astype(jnp.int32)
    running = jnp.cumsum(members, axis=0)
    position = jnp.sum(running * members, axis=1) - 1
    slot_index = owner_of * capacity + position
    placing = jnp.arange(owner_count * capacity)[:, None] == slot_index[None, :]
    outgoing = jnp.dot(
        placing.astype(jnp.bfloat16), latents, preferred_element_type=jnp.float32
    ).astype(jnp.bfloat16)
    sent_ids = jnp.max(jnp.where(placing, code_ids[None, :], -1), axis=1)
    outgoing = outgoing.reshape(host_count, local_count, capacity, latent_width)
    sent_ids = sent_ids.reshape(host_count, local_count, capacity)
    halfway = (
        lax.all_to_all(outgoing, "hst", split_axis=0, concat_axis=0, tiled=True),
        lax.all_to_all(sent_ids, "hst", split_axis=0, concat_axis=0, tiled=True),
    )
    arrived, arrived_ids = (
        lax.all_to_all(halfway[0], "local", split_axis=1, concat_axis=1, tiled=True),
        lax.all_to_all(halfway[1], "local", split_axis=1, concat_axis=1, tiled=True),
    )
    arrived = arrived.reshape(owner_count * capacity, latent_width)
    arrived_ids = arrived_ids.reshape(owner_count * capacity)
    first_code = (lax.axis_index("hst") * local_count + lax.axis_index("local")) * code_span
    offset_code = arrived_ids - first_code
    chosen = (offset_code[:, None] == jnp.arange(code_span)[None, :]).astype(jnp.bfloat16)
    code_sums = lax.dot_general(
        chosen, arrived, (((0,), (0,)), ((), ())), preferred_element_type=jnp.float32
    )
    code_counts = jnp.sum(chosen, axis=0, dtype=jnp.float32)
    new_counts = DECAY * ema_counts + (1.0 - DECAY) * code_counts
    codebook = (DECAY * ema_sums + (1.0 - DECAY) * code_sums) / new_counts[:, None]
    replies = jnp.dot(
        chosen, codebook.astype(jnp.bfloat16), preferred_element_type=jnp.float32
    ).astype(jnp.bfloat16)
    replies = replies.reshape(host_count, local_count, capacity, latent_width)
    returned = lax.all_to_all(
        lax.all_to_all(replies, "hst", split_axis=0, concat_axis=0, tiled=True),
        "local",
        split_axis=1,
        concat_axis=1,
        tiled=True,
    )
    back_rows = returned.reshape(owner_count * capacity, latent_width)
    quantized = jnp.take(back_rows, slot_index, axis=0)
    return (codebook, new_counts, quantized)


def per_device(patches, w_in, b_in, w_out, b_out, ema_sums, ema_counts, code_ids):
    hosts, locals_ = lax.axis_size("hst"), lax.axis_size("local")
    rows, span = patches.shape[0], ema_sums.shape[0]
    capacity = max(2, 2 * rows // (hosts * locals_))
    if capacity % 16 or 128 % capacity or rows != span:
        return staged(patches, w_in, b_in, w_out, b_out, ema_sums, ema_counts, code_ids)
    return fused(
        hosts, locals_, capacity,
        patches, w_in, b_in, w_out, b_out, ema_sums, ema_counts, code_ids,
    )


def solution(mesh):
    in_specs = (
        P(("hst", "local"), None),
        P(),
        P(),
        P(),
        P(),
        P(("hst", "local"), None),
        P(("hst", "local")),
        P(("hst", "local")),
    )
    out_specs = (P(("hst", "local"), None), P(("hst", "local")), P(("hst", "local"), None))
    return jax.shard_map(
        per_device, mesh=mesh, in_specs=in_specs, out_specs=out_specs, check_vma=False
    )
```

```python
import functools
import math

import jax
import jax.numpy as jnp
from jax import lax
from jax.experimental import pallas as pl
from jax.experimental.pallas import tpu as pltpu
from jax.sharding import PartitionSpec as P

DECAY = 0.9
CHUNKS = 2
DEPTH = 2
MESH = pl.DeviceIdType.MESH
F32 = jnp.float32
BF16 = jnp.bfloat16


def iota(shape, dim):
    return lax.broadcasted_iota(jnp.int32, shape, dim)


def to_column(row):
    eye = iota((128, 128), 0) == iota((128, 128), 1)
    return jnp.sum(jnp.where(eye, jnp.broadcast_to(row, (128, 128)), 0.0), axis=1, keepdims=True)


def one_hot(mask):
    return jnp.where(mask, 1.0, 0.0).astype(BF16)


def dot_nt(a, b):
    return lax.dot_general(a, b, (((1,), (1,)), ((), ())), preferred_element_type=F32)


def kernel(
    hosts, locals_, capacity,
    patches_hbm, w_in_hbm, b_in, w_out_hbm, b_out, ema_hbm, counts_row, ids_row,
    codebook, new_counts_row, quantized,
    patches, w_in, w_out, ema, hidden, latents, placing, unplacing, chosen, chosen_t, scale,
    ids_out, ids_in, out, arrived, replies, back,
    load_sem, ids_send, ids_recv, send_a, recv_a, send_b, recv_b,
):
    owners = hosts * locals_
    rows = patches.shape[0]
    span, width = ema.shape
    chunk = width // CHUNKS
    slots = owners * capacity
    group = 128 // capacity
    my_host, my_local = lax.axis_index("hst"), lax.axis_index("local")
    me = my_host * locals_ + my_local
    stride = next(k for k in range(max(1, hosts // 2 - 1), hosts + 1) if math.gcd(k, hosts) == 1)

    def each_peer(body):
        for ahead in range(1, locals_ + 1):
            local = my_local + ahead
            local = jnp.where(local >= locals_, local - locals_, local)

            def run(step, host):
                host = host + stride
                host = jnp.where(host >= hosts, host - hosts, host)
                body(host, local, host * locals_ + local)
                return host
            lax.fori_loop(0, hosts - (ahead == locals_), run, my_host)

    loads = [
        pltpu.make_async_copy(src, dst, load_sem.at[at])
        for at, (src, dst) in enumerate(
            ((patches_hbm, patches), (w_in_hbm, w_in), (w_out_hbm, w_out), (ema_hbm, ema))
        )
    ]
    for load in loads:
        load.start()
    barrier = pltpu.get_barrier_semaphore()
    each_peer(
        lambda host, local, rank: pl.semaphore_signal(
            barrier, inc=1, device_id=(host, local), device_id_type=MESH
        )
    )

    ids = ids_row[...]
    owner = ids // span
    members = iota((owners, rows), 0) == owner
    before = one_hot(iota((rows, rows), 0) <= iota((rows, rows), 1))
    running = jnp.dot(one_hot(members), before, preferred_element_type=F32)
    position = jnp.sum(jnp.where(members, running, 0.0), axis=0, keepdims=True) - 1.0
    position = position.astype(jnp.int32)
    slot = owner * capacity + position
    block = min(slots, 512)

    code = ids - owner * span + 1
    high, low = (code // 128).astype(F32), lax.rem(code, 128).astype(F32)
    line = iota((owners * 8, rows), 0) - owner * 8
    sending = jnp.where(line == 0, high, jnp.where(line == 1, low, 0.0)).astype(BF16)
    lane = position + capacity * lax.rem(me, group)
    lanes = one_hot(iota((128, rows), 0) == lane)
    ids_out[...] = dot_nt(sending, lanes).reshape(owners, 8, 128)
    ids_in[pl.ds(me, 1)] = ids_out[pl.ds(me, 1)]

    loads[0].wait()
    loads[1].wait()
    steps = slots // block
    tile = hidden.shape[1] // steps

    def first_layer(at, carry):
        columns = pl.ds(pl.multiple_of(at * tile, tile), tile)
        pre_act = jnp.dot(patches[...], w_in[:, columns], preferred_element_type=F32)
        start = pl.multiple_of(at * block, block)
        placing[pl.ds(start, block), :] = one_hot(iota((block, rows), 0) + start == slot)
        hidden[:, columns] = jnp.tanh((pre_act + b_in[:, columns]).astype(BF16))
        return carry
    lax.fori_loop(0, steps, first_layer, 0)
    loads[2].wait()

    def ids_copy(host, local, rank, slot_at):
        return pltpu.make_async_remote_copy(
            src_ref=ids_out.at[rank], dst_ref=ids_in.at[slot_at], send_sem=ids_send.at[rank],
            recv_sem=ids_recv.at[slot_at], device_id=(host, local), device_id_type=MESH,
        )

    def rows_copy(turn, host, local, rank, slot_at):
        at = turn % CHUNKS
        source, target, send, recv = (
            (out, arrived, send_a, recv_a) if turn < CHUNKS else (replies, back, send_b, recv_b)
        )
        return pltpu.make_async_remote_copy(
            src_ref=source.at[at, rank], dst_ref=target.at[at, slot_at], send_sem=send.at[at, rank],
            recv_sem=recv.at[at, slot_at], device_id=(host, local), device_id_type=MESH,
        )

    def start_turn(turn):
        def start(host, local, rank):
            if turn >= DEPTH:
                rows_copy(turn - DEPTH, host, local, rank, rank).wait_send()
            rows_copy(turn, host, local, rank, me).start()
        each_peer(start)

    def wait_turn(turn):
        each_peer(
            lambda host, local, rank: rows_copy(turn, host, local, rank, rank).wait_recv()
        )

    def send_latents(at):
        columns = slice(at * chunk, (at + 1) * chunk)
        latent = jnp.dot(hidden[...], w_out[:, columns], preferred_element_type=F32)
        latents[...] = (latent + b_out[:, columns]).astype(BF16)

        def pack(piece, carry):
            some = pl.ds(pl.multiple_of(piece * block, block), block)
            packed = jnp.dot(placing[some, :], latents[...], preferred_element_type=F32)
            count = block // capacity
            out[at, pl.ds(piece * count, count)] = packed.astype(BF16).reshape(
                count, capacity, chunk
            )
            return carry
        lax.fori_loop(0, slots // block, pack, 0)
        if at == 0:
            pl.semaphore_wait(barrier, owners - 1)
        start_turn(at)
        if at == 0:
            each_peer(lambda host, local, rank: ids_copy(host, local, rank, me).start())
        arrived[at, pl.ds(me, 1)] = out[at, pl.ds(me, 1)]

    for at in range(DEPTH):
        send_latents(at)

    for at in range(rows // 128):
        column = to_column(slot[:, at * 128:(at + 1) * 128].astype(F32)).astype(jnp.int32)
        unplacing[at * 128:(at + 1) * 128, :] = one_hot(iota((128, slots), 1) == column)

    each_peer(lambda host, local, rank: ids_copy(host, local, rank, rank).wait_recv())
    for at in range(slots // 128):
        codes = jnp.zeros((1, 128), F32)
        for source in range(at * group, (at + 1) * group):
            codes = codes + ids_in[source, 0:1, :] * 128.0 + ids_in[source, 1:2, :]
        column = to_column(codes).astype(jnp.int32)
        chosen[at * 128:(at + 1) * 128, :] = one_hot(iota((128, span), 1) + 1 == column)
        chosen_t[:, at * 128:(at + 1) * 128] = one_hot(
            iota((span, 128), 0) + 1 == codes.astype(jnp.int32)
        )
    counts = jnp.dot(jnp.ones((8, slots), BF16), chosen[...], preferred_element_type=F32)[0:1]
    new_counts = DECAY * counts_row[...] + (1.0 - DECAY) * counts
    new_counts_row[...] = new_counts
    for at in range(span // 128):
        scale[at * 128:(at + 1) * 128, :] = jnp.broadcast_to(
            to_column(new_counts[:, at * 128:(at + 1) * 128]), (128, 128)
        )
    loads[3].wait()

    for at in range(DEPTH, CHUNKS):
        send_latents(at)

    for at in range(CHUNKS):
        columns = slice(at * chunk, (at + 1) * chunk)
        wait_turn(at)
        sums = jnp.dot(
            chosen_t[...], arrived[at].reshape(slots, chunk), preferred_element_type=F32
        )
        book = (DECAY * ema[:, columns] + (1.0 - DECAY) * sums) / scale[:, 0:1]
        codebook[:, columns] = book
        latents[...] = book.astype(BF16)

        def reply(piece, carry):
            some = pl.ds(pl.multiple_of(piece * block, block), block)
            found = jnp.dot(chosen[some, :], latents[...], preferred_element_type=F32)
            count = block // capacity
            replies[at, pl.ds(piece * count, count)] = found.astype(BF16).reshape(
                count, capacity, chunk
            )
            return carry
        lax.fori_loop(0, slots // block, reply, 0)
        start_turn(CHUNKS + at)
        back[at, pl.ds(me, 1)] = replies[at, pl.ds(me, 1)]

    for at in range(CHUNKS):
        columns = slice(at * chunk, (at + 1) * chunk)
        if at == CHUNKS - 1:
            each_peer(lambda host, local, rank: ids_copy(host, local, rank, rank).wait_send())
            for turn in range(2 * CHUNKS - DEPTH, 2 * CHUNKS):
                each_peer(
                    lambda host, local, rank: rows_copy(turn, host, local, rank, rank).wait_send()
                )
        wait_turn(CHUNKS + at)
        quantized[:, columns] = jnp.dot(
            unplacing[...], back[at].reshape(slots, chunk), preferred_element_type=F32
        ).astype(BF16)


def fused(hosts, locals_, capacity, patches, w_in, b_in, w_out, b_out, ema_sums, ema_counts, code_ids):
    owners = hosts * locals_
    rows, depth = patches.shape
    span, width = ema_sums.shape
    hidden = w_in.shape[1]
    chunk = width // CHUNKS
    slots = owners * capacity
    vmem = pl.BlockSpec(memory_space=pltpu.VMEM)
    hbm = pl.BlockSpec(memory_space=pl.ANY)
    traded = pltpu.VMEM((CHUNKS, owners, capacity, chunk), BF16)
    dma = pltpu.SemaphoreType.DMA
    flops = 2 * rows * hidden * (depth + width) + 8 * slots * rows * width
    codebook, new_counts, quantized = pl.pallas_call(
        functools.partial(kernel, hosts, locals_, capacity),
        out_shape=(
            pltpu.VMEM((span, width), F32),
            jax.ShapeDtypeStruct((1, span), F32),
            pltpu.VMEM((rows, width), BF16),
        ),
        in_specs=[hbm, hbm, vmem, hbm, vmem, hbm, vmem, vmem],
        out_specs=(vmem, vmem, vmem),
        scratch_shapes=[
            pltpu.VMEM((rows, depth), BF16),
            pltpu.VMEM((depth, hidden), BF16),
            pltpu.VMEM((hidden, width), BF16),
            pltpu.VMEM((span, width), F32),
            pltpu.VMEM((rows, hidden), BF16),
            pltpu.VMEM((max(rows, span), chunk), BF16),
            pltpu.VMEM((slots, rows), BF16),
            pltpu.VMEM((rows, slots), BF16),
            pltpu.VMEM((slots, span), BF16),
            pltpu.VMEM((span, slots), BF16),
            pltpu.VMEM((span, 128), F32),
            pltpu.VMEM((owners, 8, 128), F32),
            pltpu.VMEM((owners, 8, 128), F32),
            traded, traded, traded, traded,
            dma((4,)), dma((owners,)), dma((owners,)),
            dma((CHUNKS, owners)), dma((CHUNKS, owners)),
            dma((CHUNKS, owners)), dma((CHUNKS, owners)),
        ],
        compiler_params=pltpu.CompilerParams(
            collective_id=0, has_side_effects=True, vmem_limit_bytes=56 * 2**20
        ),
        cost_estimate=pl.CostEstimate(
            flops=flops, bytes_accessed=14 * 2**20, transcendentals=rows * hidden
        ),
    )(
        patches, w_in, b_in.reshape(1, -1), w_out, b_out.reshape(1, -1), ema_sums,
        ema_counts.reshape(1, -1), code_ids.reshape(1, -1),
    )
    return codebook, new_counts.reshape(span), quantized


def staged(patches, w_in, b_in, w_out, b_out, ema_sums, ema_counts, code_ids):
    host_count = lax.axis_size("hst")
    local_count = lax.axis_size("local")
    owner_count = host_count * local_count
    code_span = ema_sums.shape[0]
    latent_width = ema_sums.shape[1]
    row_count = patches.shape[0]
    capacity = max(2, 2 * row_count // owner_count)
    pre_act = jnp.dot(patches, w_in, preferred_element_type=jnp.float32) + b_in
    hidden = jnp.tanh(pre_act).astype(jnp.bfloat16)
    latents = (jnp.dot(hidden, w_out, preferred_element_type=jnp.float32) + b_out).astype(
        jnp.bfloat16
    )
    owner_of = code_ids // code_span
    members = (owner_of[:, None] == jnp.arange(owner_count)[None, :]).astype(jnp.int32)
    running = jnp.cumsum(members, axis=0)
    position = jnp.sum(running * members, axis=1) - 1
    slot_index = owner_of * capacity + position
    placing = jnp.arange(owner_count * capacity)[:, None] == slot_index[None, :]
    outgoing = jnp.dot(
        placing.astype(jnp.bfloat16), latents, preferred_element_type=jnp.float32
    ).astype(jnp.bfloat16)
    sent_ids = jnp.max(jnp.where(placing, code_ids[None, :], -1), axis=1)
    outgoing = outgoing.reshape(host_count, local_count, capacity, latent_width)
    sent_ids = sent_ids.reshape(host_count, local_count, capacity)
    halfway = (
        lax.all_to_all(outgoing, "hst", split_axis=0, concat_axis=0, tiled=True),
        lax.all_to_all(sent_ids, "hst", split_axis=0, concat_axis=0, tiled=True),
    )
    arrived, arrived_ids = (
        lax.all_to_all(halfway[0], "local", split_axis=1, concat_axis=1, tiled=True),
        lax.all_to_all(halfway[1], "local", split_axis=1, concat_axis=1, tiled=True),
    )
    arrived = arrived.reshape(owner_count * capacity, latent_width)
    arrived_ids = arrived_ids.reshape(owner_count * capacity)
    first_code = (lax.axis_index("hst") * local_count + lax.axis_index("local")) * code_span
    offset_code = arrived_ids - first_code
    chosen = (offset_code[:, None] == jnp.arange(code_span)[None, :]).astype(jnp.bfloat16)
    code_sums = lax.dot_general(
        chosen, arrived, (((0,), (0,)), ((), ())), preferred_element_type=jnp.float32
    )
    code_counts = jnp.sum(chosen, axis=0, dtype=jnp.float32)
    new_counts = DECAY * ema_counts + (1.0 - DECAY) * code_counts
    codebook = (DECAY * ema_sums + (1.0 - DECAY) * code_sums) / new_counts[:, None]
    replies = jnp.dot(
        chosen, codebook.astype(jnp.bfloat16), preferred_element_type=jnp.float32
    ).astype(jnp.bfloat16)
    replies = replies.reshape(host_count, local_count, capacity, latent_width)
    returned = lax.all_to_all(
        lax.all_to_all(replies, "hst", split_axis=0, concat_axis=0, tiled=True),
        "local",
        split_axis=1,
        concat_axis=1,
        tiled=True,
    )
    back_rows = returned.reshape(owner_count * capacity, latent_width)
    quantized = jnp.take(back_rows, slot_index, axis=0)
    return (codebook, new_counts, quantized)


def per_device(patches, w_in, b_in, w_out, b_out, ema_sums, ema_counts, code_ids):
    hosts, locals_ = lax.axis_size("hst"), lax.axis_size("local")
    rows, span = patches.shape[0], ema_sums.shape[0]
    capacity = max(2, 2 * rows // (hosts * locals_))
    slots = hosts * locals_ * capacity
    if capacity % 16 or 128 % capacity or rows != span or slots % 512:
        return staged(patches, w_in, b_in, w_out, b_out, ema_sums, ema_counts, code_ids)
    return fused(
        hosts, locals_, capacity,
        patches, w_in, b_in, w_out, b_out, ema_sums, ema_counts, code_ids,
    )


def solution(mesh):
    in_specs = (
        P(("hst", "local"), None),
        P(),
        P(),
        P(),
        P(),
        P(("hst", "local"), None),
        P(("hst", "local")),
        P(("hst", "local")),
    )
    out_specs = (P(("hst", "local"), None), P(("hst", "local")), P(("hst", "local"), None))
    return jax.shard_map(
        per_device, mesh=mesh, in_specs=in_specs, out_specs=out_specs, check_vma=False
    )
```

```python
import functools
import math

import jax
import jax.numpy as jnp
from jax import lax
from jax.experimental import pallas as pl
from jax.experimental.pallas import tpu as pltpu
from jax.sharding import PartitionSpec as P

DECAY = 0.9
CHUNKS = 2
DEPTH = 2
MESH = pl.DeviceIdType.MESH
F32 = jnp.float32
BF16 = jnp.bfloat16


def iota(shape, dim):
    return lax.broadcasted_iota(jnp.int32, shape, dim)


def to_column(row):
    eye = iota((128, 128), 0) == iota((128, 128), 1)
    return jnp.sum(jnp.where(eye, jnp.broadcast_to(row, (128, 128)), 0.0), axis=1, keepdims=True)


def one_hot(mask):
    return jnp.where(mask, 1.0, 0.0).astype(BF16)


def dot_nt(a, b):
    return lax.dot_general(a, b, (((1,), (1,)), ((), ())), preferred_element_type=F32)


def kernel(
    hosts, locals_, capacity,
    patches_hbm, w_in_hbm, b_in, w_out_hbm, b_out, ema_hbm, counts_row, ids_row,
    codebook, new_counts_row, quantized,
    patches, w_in, w_out, ema, hidden, latents, placing, unplacing, chosen, chosen_t, scale,
    ids_out, ids_in, out, arrived, replies, back,
    load_sem, ids_send, ids_recv, send_a, recv_a, send_b, recv_b,
):
    owners = hosts * locals_
    rows = patches.shape[0]
    span, width = ema.shape
    chunk = width // CHUNKS
    slots = owners * capacity
    group = 128 // capacity
    my_host, my_local = lax.axis_index("hst"), lax.axis_index("local")
    me = my_host * locals_ + my_local
    stride = next(k for k in range(max(1, hosts // 2 - 1), hosts + 1) if math.gcd(k, hosts) == 1)

    def each_peer(body):
        for ahead in range(1, locals_ + 1):
            local = my_local + ahead
            local = jnp.where(local >= locals_, local - locals_, local)

            def run(step, host):
                host = host + stride
                host = jnp.where(host >= hosts, host - hosts, host)
                body(host, local, host * locals_ + local)
                return host
            lax.fori_loop(0, hosts - (ahead == locals_), run, my_host)

    loads = [
        pltpu.make_async_copy(src, dst, load_sem.at[at])
        for at, (src, dst) in enumerate(
            ((patches_hbm, patches), (w_in_hbm, w_in), (w_out_hbm, w_out), (ema_hbm, ema))
        )
    ]
    for load in loads:
        load.start()
    barrier = pltpu.get_barrier_semaphore()
    each_peer(
        lambda host, local, rank: pl.semaphore_signal(
            barrier, inc=1, device_id=(host, local), device_id_type=MESH
        )
    )

    ids = ids_row[...]
    owner = ids // span
    members = iota((owners, rows), 0) == owner
    before = one_hot(iota((rows, rows), 0) <= iota((rows, rows), 1))
    running = jnp.dot(one_hot(members), before, preferred_element_type=F32)
    position = jnp.sum(jnp.where(members, running, 0.0), axis=0, keepdims=True) - 1.0
    position = position.astype(jnp.int32)
    slot = owner * capacity + position
    block = min(slots, 512)

    loads[0].wait()
    loads[1].wait()
    steps = slots // block
    tile = hidden.shape[1] // steps

    def first_layer(at, carry):
        columns = pl.ds(pl.multiple_of(at * tile, tile), tile)
        pre_act = jnp.dot(patches[...], w_in[:, columns], preferred_element_type=F32)
        start = pl.multiple_of(at * block, block)
        placing[pl.ds(start, block), :] = one_hot(iota((block, rows), 0) + start == slot)
        hidden[:, columns] = jnp.tanh((pre_act + b_in[:, columns]).astype(BF16))
        return carry
    lax.fori_loop(0, steps, first_layer, 0)
    loads[2].wait()

    def pack_ids():
        code = ids - owner * span + 1
        high, low = (code // 128).astype(F32), lax.rem(code, 128).astype(F32)
        line = iota((owners * 8, rows), 0) - owner * 8
        sending = jnp.where(line == 0, high, jnp.where(line == 1, low, 0.0)).astype(BF16)
        lane = position + capacity * lax.rem(me, group)
        lanes = one_hot(iota((128, rows), 0) == lane)
        ids_out[...] = dot_nt(sending, lanes).reshape(owners, 8, 128)
        ids_in[pl.ds(me, 1)] = ids_out[pl.ds(me, 1)]

    def ids_copy(host, local, rank, slot_at):
        return pltpu.make_async_remote_copy(
            src_ref=ids_out.at[rank], dst_ref=ids_in.at[slot_at], send_sem=ids_send.at[rank],
            recv_sem=ids_recv.at[slot_at], device_id=(host, local), device_id_type=MESH,
        )

    def rows_copy(turn, host, local, rank, slot_at):
        at = turn % CHUNKS
        source, target, send, recv = (
            (out, arrived, send_a, recv_a) if turn < CHUNKS else (replies, back, send_b, recv_b)
        )
        return pltpu.make_async_remote_copy(
            src_ref=source.at[at, rank], dst_ref=target.at[at, slot_at], send_sem=send.at[at, rank],
            recv_sem=recv.at[at, slot_at], device_id=(host, local), device_id_type=MESH,
        )

    def start_turn(turn):
        def start(host, local, rank):
            if turn >= DEPTH:
                rows_copy(turn - DEPTH, host, local, rank, rank).wait_send()
            rows_copy(turn, host, local, rank, me).start()
        each_peer(start)

    def wait_turn(turn):
        each_peer(
            lambda host, local, rank: rows_copy(turn, host, local, rank, rank).wait_recv()
        )

    def send_latents(at):
        columns = slice(at * chunk, (at + 1) * chunk)
        latent = jnp.dot(hidden[...], w_out[:, columns], preferred_element_type=F32)
        latents[...] = (latent + b_out[:, columns]).astype(BF16)

        def pack(piece, carry):
            some = pl.ds(pl.multiple_of(piece * block, block), block)
            packed = jnp.dot(placing[some, :], latents[...], preferred_element_type=F32)
            count = block // capacity
            out[at, pl.ds(piece * count, count)] = packed.astype(BF16).reshape(
                count, capacity, chunk
            )
            return carry
        lax.fori_loop(0, slots // block, pack, 0)
        if at == 0:
            pl.semaphore_wait(barrier, owners - 1)
        start_turn(at)
        if at == 0:
            pack_ids()
            each_peer(lambda host, local, rank: ids_copy(host, local, rank, me).start())
        arrived[at, pl.ds(me, 1)] = out[at, pl.ds(me, 1)]

    for at in range(DEPTH):
        send_latents(at)

    for at in range(rows // 128):
        column = to_column(slot[:, at * 128:(at + 1) * 128].astype(F32)).astype(jnp.int32)
        unplacing[at * 128:(at + 1) * 128, :] = one_hot(iota((128, slots), 1) == column)

    each_peer(lambda host, local, rank: ids_copy(host, local, rank, rank).wait_recv())
    for at in range(slots // 128):
        codes = jnp.zeros((1, 128), F32)
        for source in range(at * group, (at + 1) * group):
            codes = codes + ids_in[source, 0:1, :] * 128.0 + ids_in[source, 1:2, :]
        column = to_column(codes).astype(jnp.int32)
        chosen[at * 128:(at + 1) * 128, :] = one_hot(iota((128, span), 1) + 1 == column)
        chosen_t[:, at * 128:(at + 1) * 128] = one_hot(
            iota((span, 128), 0) + 1 == codes.astype(jnp.int32)
        )
    counts = jnp.dot(jnp.ones((8, slots), BF16), chosen[...], preferred_element_type=F32)[0:1]
    new_counts = DECAY * counts_row[...] + (1.0 - DECAY) * counts
    new_counts_row[...] = new_counts
    for at in range(span // 128):
        scale[at * 128:(at + 1) * 128, :] = jnp.broadcast_to(
            to_column(new_counts[:, at * 128:(at + 1) * 128]), (128, 128)
        )
    loads[3].wait()

    for at in range(DEPTH, CHUNKS):
        send_latents(at)

    for at in range(CHUNKS):
        columns = slice(at * chunk, (at + 1) * chunk)
        wait_turn(at)
        sums = jnp.dot(
            chosen_t[...], arrived[at].reshape(slots, chunk), preferred_element_type=F32
        )
        book = (DECAY * ema[:, columns] + (1.0 - DECAY) * sums) / scale[:, 0:1]
        codebook[:, columns] = book
        latents[...] = book.astype(BF16)

        def reply(piece, carry):
            some = pl.ds(pl.multiple_of(piece * block, block), block)
            found = jnp.dot(chosen[some, :], latents[...], preferred_element_type=F32)
            count = block // capacity
            replies[at, pl.ds(piece * count, count)] = found.astype(BF16).reshape(
                count, capacity, chunk
            )
            return carry
        lax.fori_loop(0, slots // block, reply, 0)
        start_turn(CHUNKS + at)
        back[at, pl.ds(me, 1)] = replies[at, pl.ds(me, 1)]

    for at in range(CHUNKS):
        columns = slice(at * chunk, (at + 1) * chunk)
        if at == CHUNKS - 1:
            each_peer(lambda host, local, rank: ids_copy(host, local, rank, rank).wait_send())
            for turn in range(2 * CHUNKS - DEPTH, 2 * CHUNKS):
                each_peer(
                    lambda host, local, rank: rows_copy(turn, host, local, rank, rank).wait_send()
                )
        wait_turn(CHUNKS + at)
        quantized[:, columns] = jnp.dot(
            unplacing[...], back[at].reshape(slots, chunk), preferred_element_type=F32
        ).astype(BF16)


def fused(hosts, locals_, capacity, patches, w_in, b_in, w_out, b_out, ema_sums, ema_counts, code_ids):
    owners = hosts * locals_
    rows, depth = patches.shape
    span, width = ema_sums.shape
    hidden = w_in.shape[1]
    chunk = width // CHUNKS
    slots = owners * capacity
    vmem = pl.BlockSpec(memory_space=pltpu.VMEM)
    hbm = pl.BlockSpec(memory_space=pl.ANY)
    traded = pltpu.VMEM((CHUNKS, owners, capacity, chunk), BF16)
    dma = pltpu.SemaphoreType.DMA
    flops = 2 * rows * hidden * (depth + width) + 8 * slots * rows * width
    codebook, new_counts, quantized = pl.pallas_call(
        functools.partial(kernel, hosts, locals_, capacity),
        out_shape=(
            pltpu.VMEM((span, width), F32),
            jax.ShapeDtypeStruct((1, span), F32),
            pltpu.VMEM((rows, width), BF16),
        ),
        in_specs=[hbm, hbm, vmem, hbm, vmem, hbm, vmem, vmem],
        out_specs=(vmem, vmem, vmem),
        scratch_shapes=[
            pltpu.VMEM((rows, depth), BF16),
            pltpu.VMEM((depth, hidden), BF16),
            pltpu.VMEM((hidden, width), BF16),
            pltpu.VMEM((span, width), F32),
            pltpu.VMEM((rows, hidden), BF16),
            pltpu.VMEM((max(rows, span), chunk), BF16),
            pltpu.VMEM((slots, rows), BF16),
            pltpu.VMEM((rows, slots), BF16),
            pltpu.VMEM((slots, span), BF16),
            pltpu.VMEM((span, slots), BF16),
            pltpu.VMEM((span, 128), F32),
            pltpu.VMEM((owners, 8, 128), F32),
            pltpu.VMEM((owners, 8, 128), F32),
            traded, traded, traded, traded,
            dma((4,)), dma((owners,)), dma((owners,)),
            dma((CHUNKS, owners)), dma((CHUNKS, owners)),
            dma((CHUNKS, owners)), dma((CHUNKS, owners)),
        ],
        compiler_params=pltpu.CompilerParams(
            collective_id=0, has_side_effects=True, vmem_limit_bytes=56 * 2**20
        ),
        cost_estimate=pl.CostEstimate(
            flops=flops, bytes_accessed=14 * 2**20, transcendentals=rows * hidden
        ),
    )(
        patches, w_in, b_in.reshape(1, -1), w_out, b_out.reshape(1, -1), ema_sums,
        ema_counts.reshape(1, -1), code_ids.reshape(1, -1),
    )
    return codebook, new_counts.reshape(span), quantized


def staged(patches, w_in, b_in, w_out, b_out, ema_sums, ema_counts, code_ids):
    host_count = lax.axis_size("hst")
    local_count = lax.axis_size("local")
    owner_count = host_count * local_count
    code_span = ema_sums.shape[0]
    latent_width = ema_sums.shape[1]
    row_count = patches.shape[0]
    capacity = max(2, 2 * row_count // owner_count)
    pre_act = jnp.dot(patches, w_in, preferred_element_type=jnp.float32) + b_in
    hidden = jnp.tanh(pre_act).astype(jnp.bfloat16)
    latents = (jnp.dot(hidden, w_out, preferred_element_type=jnp.float32) + b_out).astype(
        jnp.bfloat16
    )
    owner_of = code_ids // code_span
    members = (owner_of[:, None] == jnp.arange(owner_count)[None, :]).astype(jnp.int32)
    running = jnp.cumsum(members, axis=0)
    position = jnp.sum(running * members, axis=1) - 1
    slot_index = owner_of * capacity + position
    placing = jnp.arange(owner_count * capacity)[:, None] == slot_index[None, :]
    outgoing = jnp.dot(
        placing.astype(jnp.bfloat16), latents, preferred_element_type=jnp.float32
    ).astype(jnp.bfloat16)
    sent_ids = jnp.max(jnp.where(placing, code_ids[None, :], -1), axis=1)
    outgoing = outgoing.reshape(host_count, local_count, capacity, latent_width)
    sent_ids = sent_ids.reshape(host_count, local_count, capacity)
    halfway = (
        lax.all_to_all(outgoing, "hst", split_axis=0, concat_axis=0, tiled=True),
        lax.all_to_all(sent_ids, "hst", split_axis=0, concat_axis=0, tiled=True),
    )
    arrived, arrived_ids = (
        lax.all_to_all(halfway[0], "local", split_axis=1, concat_axis=1, tiled=True),
        lax.all_to_all(halfway[1], "local", split_axis=1, concat_axis=1, tiled=True),
    )
    arrived = arrived.reshape(owner_count * capacity, latent_width)
    arrived_ids = arrived_ids.reshape(owner_count * capacity)
    first_code = (lax.axis_index("hst") * local_count + lax.axis_index("local")) * code_span
    offset_code = arrived_ids - first_code
    chosen = (offset_code[:, None] == jnp.arange(code_span)[None, :]).astype(jnp.bfloat16)
    code_sums = lax.dot_general(
        chosen, arrived, (((0,), (0,)), ((), ())), preferred_element_type=jnp.float32
    )
    code_counts = jnp.sum(chosen, axis=0, dtype=jnp.float32)
    new_counts = DECAY * ema_counts + (1.0 - DECAY) * code_counts
    codebook = (DECAY * ema_sums + (1.0 - DECAY) * code_sums) / new_counts[:, None]
    replies = jnp.dot(
        chosen, codebook.astype(jnp.bfloat16), preferred_element_type=jnp.float32
    ).astype(jnp.bfloat16)
    replies = replies.reshape(host_count, local_count, capacity, latent_width)
    returned = lax.all_to_all(
        lax.all_to_all(replies, "hst", split_axis=0, concat_axis=0, tiled=True),
        "local",
        split_axis=1,
        concat_axis=1,
        tiled=True,
    )
    back_rows = returned.reshape(owner_count * capacity, latent_width)
    quantized = jnp.take(back_rows, slot_index, axis=0)
    return (codebook, new_counts, quantized)


def per_device(patches, w_in, b_in, w_out, b_out, ema_sums, ema_counts, code_ids):
    hosts, locals_ = lax.axis_size("hst"), lax.axis_size("local")
    rows, span = patches.shape[0], ema_sums.shape[0]
    capacity = max(2, 2 * rows // (hosts * locals_))
    slots = hosts * locals_ * capacity
    if capacity % 16 or 128 % capacity or rows != span or slots % 512:
        return staged(patches, w_in, b_in, w_out, b_out, ema_sums, ema_counts, code_ids)
    return fused(
        hosts, locals_, capacity,
        patches, w_in, b_in, w_out, b_out, ema_sums, ema_counts, code_ids,
    )


def solution(mesh):
    in_specs = (
        P(("hst", "local"), None),
        P(),
        P(),
        P(),
        P(),
        P(("hst", "local"), None),
        P(("hst", "local")),
        P(("hst", "local")),
    )
    out_specs = (P(("hst", "local"), None), P(("hst", "local")), P(("hst", "local"), None))
    return jax.shard_map(
        per_device, mesh=mesh, in_specs=in_specs, out_specs=out_specs, check_vma=False
    )
```
